512 devices in a mesh: rep: 16 (over z_hi, y, core), fsdp: 32 (over z_lo, x).
Axes of the slice: x: 4, y: 4, z: 16 (z_hi: 2, z_lo: 8; z = z_hi * 8 + z_lo), core: 2. Of those that a mesh axis runs over, the one named last changes fastest.
Arguments:
- base_weights: bfloat16 [28672, 832], P('fsdp'), may hold values from -6 to 6
- local_weights: bfloat16 [16, 28672, 832], P('rep', 'fsdp'), may hold values from -6 to 6
- momentum: float32 [28672, 832], P(('fsdp', 'rep')), may hold values from -6 to 6
- sketch_matrix: bfloat16 [28672, 512], P(('fsdp', 'rep')), may hold values from -0.25 to 0.25
Outputs:
- new_weights: bfloat16 [28672, 832], P('fsdp')
- new_momentum: float32 [28672, 832], P(('fsdp', 'rep'))
The draws below stay inside these ranges and needn't reach their ends.
All inputs are finite; a program needn't handle non-finite values.
Results may differ from the reference program's by a relative error of at most 0.00115.
Values may be sent and summed in bfloat16 or wider, within the bound.
No kernel may reach another device: no remote copies, remote signals or barrier semaphores. Data moves between devices by JAX's collectives and lax.ppermute only.
A program may use at most 64 MiB of HBM per device.

```python
import jax
import jax.numpy as jnp
from jax import lax

FF = 28672
RANK = 512
SLAB = 832
REPS = 16


def strengthened(array, key, source, target, parts, factor):
    def block_of(axis_at):
        return (jnp.arange(array.shape[axis_at]) // (array.shape[axis_at] // parts)).reshape((-1,) + (1,) * (array.ndim - 1 - axis_at))

    first = jax.random.permutation(key, parts)[block_of(target)]
    other_side = (block_of(target) + parts // 2) % parts
    return jnp.where((block_of(source) == first) | (block_of(source) == other_side), factor * array, array)


def block_levels(own_key, extent, cuts, smallest, largest):
    loudness, own = 1.0, jax.random.fold_in(own_key, 6)
    for axis_at, blocks in cuts:
        draws = jnp.exp(jax.random.uniform(jax.random.fold_in(own, axis_at), (blocks,), jnp.float32, smallest / len(cuts), largest / len(cuts)))
        loudness = loudness * jnp.repeat(draws, extent[axis_at] // blocks).reshape([-1 if axis == axis_at else 1 for axis in range(len(extent))])
    return loudness


def scatter_about(own_key, shape, scale, bound, shards=(), kind=jnp.bfloat16):
    loudness = block_levels(own_key, shape, shards, -0.22, 0.18) if shards else 1.0
    drawn = jax.random.normal(own_key, shape, jnp.float32) * scale * loudness
    return jnp.minimum(jnp.maximum(drawn, -bound), bound).astype(kind)


def gaussian_with(stream_key, dims, deviation, limit, pieces, heavy, held_as=jnp.bfloat16):
    values = deviation * jax.random.normal(stream_key, dims, jnp.float32)
    if pieces:
        values = values * block_levels(stream_key, dims, pieces, -0.22, 0.18)
    return jnp.clip(strengthened(values, jax.random.fold_in(stream_key, 3), *heavy), -limit, limit).astype(held_as)


def setup_inputs(seed: int = 0) -> dict:
    key_of = jax.random.split(jax.random.key(seed), 5)
    base_weights = scatter_about(key_of[0], (FF, SLAB), 1.0, 6.0, ((0, 32),))
    local_weights = gaussian_with(key_of[1], (REPS, FF, SLAB), 1.0, 6.0, ((0, 16), (1, 32)), (0, 1, 16, 2.0))
    momentum = scatter_about(key_of[2], (FF, SLAB), 1.0, 6.0, ((0, 512),), jnp.float32)
    sketch_matrix = scatter_about(key_of[3], (FF, RANK), RANK ** -0.5, 0.25, ((0, 512),))
    return {"base_weights": base_weights, "local_weights": local_weights, "momentum": momentum, "sketch_matrix": sketch_matrix}


def reference(base_weights, local_weights, momentum, sketch_matrix):
    base_wide = base_weights.astype(jnp.float32)

    def add_group(total, local_one):
        return total + (base_wide - local_one.astype(jnp.float32)), None

    drift_total, unused = lax.scan(add_group, jnp.zeros(base_wide.shape, jnp.float32), local_weights)
    gauss = sketch_matrix.astype(jnp.float32)
    sketch = jnp.dot(gauss.T, drift_total, precision=lax.Precision.HIGHEST, preferred_element_type=jnp.float32) / REPS
    decoded = jnp.dot(gauss, sketch, precision=lax.Precision.HIGHEST, preferred_element_type=jnp.float32)
    new_momentum = 0.9 * momentum + decoded
    new_weights = (base_wide - 0.7 * (decoded + 0.9 * new_momentum)).astype(jnp.bfloat16)
    return new_weights, new_momentum
```

```python
import jax
import jax.numpy as jnp
import numpy as np
from jax import lax
from jax.sharding import Mesh, PartitionSpec as P

REP = ("zhi", "y", "core")
FSDP = ("zlo", "x")
PLANE = ("y", "core")
SUMMED = ("zhi", "zlo", "x")
ALL = REP + FSDP
SIZES = (2, 4, 2, 8, 4)
GROUPS = 16
CUTS = 8
HIGHEST = lax.Precision.HIGHEST


def swapped(axis):
    index = np.arange(int(np.prod(SIZES))).reshape(SIZES)
    other = np.flip(index, axis=ALL.index(axis))
    return [(int(a), int(b)) for a, b in zip(index.ravel(), other.ravel())]


def swap(value, axis):
    return lax.ppermute(value, ALL, swapped(axis))


def in_order(own, other, axis, at):
    first = lax.axis_index(axis) == 0
    return jnp.stack([jnp.where(first, own, other), jnp.where(first, other, own)], axis=at)


def spread(value, axes, parts):
    return lax.all_to_all(jnp.broadcast_to(value[None], (parts,) + value.shape), axes, 0, 0, tiled=True)


def shards(base_weights, local_weights, momentum, sketch_matrix):
    rows, width = momentum.shape
    rank = sketch_matrix.shape[1]
    cols = width // CUTS
    held = base_weights.shape[0]
    cut = lax.axis_index(PLANE)

    with jax.named_scope("sketch_rows_zhi"):
        sketch_pair = in_order(sketch_matrix, swap(sketch_matrix, "zhi"), "zhi", 0)
    with jax.named_scope("momentum_rows_zhi"):
        momentum_pair = in_order(momentum, swap(momentum, "zhi"), "zhi", 0)
    with jax.named_scope("local_columns"):
        local_cols = lax.all_to_all(local_weights[0].T.reshape(CUTS, cols, held), PLANE, 0, 0, tiled=True)
    with jax.named_scope("sketch_rows_plane"):
        gathered = lax.all_gather(sketch_pair.reshape(2 * rows, rank), PLANE, axis=0, tiled=False)
        gauss = gathered.reshape(CUTS, 2, rows, rank).transpose(1, 0, 2, 3).reshape(held, rank).astype(jnp.float32)
    with jax.named_scope("momentum_columns"):
        pieces = momentum_pair.reshape(2 * rows, CUTS, cols).transpose(1, 0, 2)
        pieces = lax.all_to_all(pieces, PLANE, 0, 0, tiled=True).reshape(CUTS, 2, rows, cols)
        momentum_cols = pieces.transpose(1, 0, 2, 3).reshape(held, cols).T
    with jax.named_scope("drift"):
        base_cols = lax.dynamic_slice_in_dim(base_weights.T, cut * cols, cols, 0).astype(jnp.float32)
        drift = jnp.sum(base_cols[None] - local_cols.astype(jnp.float32), axis=0)
    with jax.named_scope("partial_sketch"):
        partial = jnp.dot(drift, gauss, precision=HIGHEST, preferred_element_type=jnp.float32)
    with jax.named_scope("sketch_sum"):
        padded = jnp.pad(partial, ((0, 128 - cols), (0, 0)))
        tiles = padded.reshape(16, 8, 4, 128).transpose(0, 2, 1, 3).reshape(64, 8, 128)
        mine = jnp.sum(lax.all_to_all(tiles, SUMMED, 0, 0, tiled=True), axis=0)
        tiles = spread(mine, SUMMED, 64).reshape(16, 4, 8, 128)
        sketch = tiles.transpose(0, 2, 1, 3).reshape(128, rank)[:cols] / GROUPS
    with jax.named_scope("decode"):
        decoded = lax.dot_general(
            sketch, gauss, (((1,), (1,)), ((), ())), precision=HIGHEST, preferred_element_type=jnp.float32
        )
        stepped = 0.9 * momentum_cols + decoded
        updated = (base_cols - 0.7 * (decoded + 0.9 * stepped)).astype(jnp.bfloat16)
    with jax.named_scope("weights_y"):
        over_y = spread(updated, "y", 4)
    with jax.named_scope("weights_core"):
        both = in_order(over_y, swap(over_y, "core"), "core", 1)
        new_weights = both.reshape(width, held).T
    with jax.named_scope("decoded_rows"):
        plane_rows = lax.dynamic_slice_in_dim(decoded, lax.axis_index("zhi") * (held // 2), held // 2, 1)
        plane_rows = plane_rows.T.reshape(CUTS, rows, cols)
        back = lax.all_to_all(plane_rows, PLANE, 0, 0, tiled=True)
        new_momentum = 0.9 * momentum + back.transpose(1, 0, 2).reshape(rows, width)
    return new_weights, new_momentum


def solution(mesh):
    fine = Mesh(mesh.devices.reshape(SIZES), ALL)
    placed = (P(FSDP, None), P(REP, FSDP, None), P(FSDP + REP, None), P(FSDP + REP, None))
    return jax.shard_map(
        shards,
        mesh=fine,
        in_specs=placed,
        out_specs=(P(FSDP, None), P(FSDP + REP, None)),
        check_vma=False,
    )
```

```python
import jax
import jax.numpy as jnp
import numpy as np
from jax import lax
from jax.sharding import Mesh, PartitionSpec as P

REP = ("zhi", "y", "core")
FSDP = ("zm", "zn", "x")
PLANE = ("y", "core")
NEAR = ("zn", "x")
FAR = ("zhi", "zm")
ALL = REP + FSDP
SIZES = (2, 4, 2, 2, 4, 4)
GROUPS = 16
CUTS = 8
HIGHEST = lax.Precision.HIGHEST


def swapped(axis):
    index = np.arange(int(np.prod(SIZES))).reshape(SIZES)
    other = np.flip(index, axis=ALL.index(axis))
    return [(int(a), int(b)) for a, b in zip(index.ravel(), other.ravel())]


def swap(value, axis):
    return lax.ppermute(value, ALL, swapped(axis))


def in_order(own, other, axis, at):
    first = lax.axis_index(axis) == 0
    return jnp.stack([jnp.where(first, own, other), jnp.where(first, other, own)], axis=at)


def spread(value, axes, parts):
    return lax.all_to_all(jnp.broadcast_to(value[None], (parts,) + value.shape), axes, 0, 0, tiled=True)


def halves(value):
    high = lax.reduce_precision(value, 8, 7)
    return high.astype(jnp.bfloat16), (value - high).astype(jnp.bfloat16)


def joined(high, low):
    return high.astype(jnp.float32) + low.astype(jnp.float32)


def wide(value, lanes):
    return jnp.pad(value, [(0, 0)] * (value.ndim - 1) + [(0, lanes - value.shape[-1])])


def shards(base_weights, local_weights, momentum, sketch_matrix):
    rows, width = momentum.shape
    rank = sketch_matrix.shape[1]
    cols = width // CUTS
    held = base_weights.shape[0]
    cut = lax.axis_index(PLANE)

    with jax.named_scope("sketch_rows_zhi"):
        sketch_pair = in_order(sketch_matrix, swap(sketch_matrix, "zhi"), "zhi", 0)
    with jax.named_scope("local_and_momentum_columns"):
        high, low = halves(momentum.T)
        sent = jnp.concatenate([local_weights[0].T, high, low], axis=1)
        got = lax.all_to_all(wide(sent, 1024).reshape(CUTS, cols, 1024), PLANE, 0, 0, tiled=True)
    with jax.named_scope("sketch_rows_plane"):
        gathered = lax.all_gather(sketch_pair.reshape(2 * rows, rank), PLANE, axis=0, tiled=False)
        gauss = gathered.reshape(CUTS, 2, rows, rank).transpose(1, 0, 2, 3).reshape(held, rank).astype(jnp.float32)
    with jax.named_scope("drift"):
        base_cols = lax.dynamic_slice_in_dim(base_weights.T, cut * cols, cols, 0).astype(jnp.float32)
        drift = jnp.sum(base_cols[None] - got[:, :, :held].astype(jnp.float32), axis=0)
    with jax.named_scope("partial_sketch"):
        partial = jnp.dot(drift, gauss, precision=HIGHEST, preferred_element_type=jnp.float32)
    with jax.named_scope("momentum_columns_zhi"):
        own = joined(got[:, :, held : held + rows], got[:, :, held + rows : held + 2 * rows])
        own = own.transpose(1, 0, 2).reshape(cols, held // 2)
        other = swap((own * 8192.0).astype(jnp.float16), "zhi").astype(jnp.float32) / 8192.0
        momentum_cols = in_order(own, other, "zhi", 1).reshape(cols, held)
    with jax.named_scope("sketch_sum"):
        padded = jnp.pad(partial, ((0, 128 - cols), (0, 0)))
        mine = jnp.sum(lax.all_to_all(padded.reshape(16, 8, rank), NEAR, 0, 0, tiled=True), axis=0)
        mine = jnp.sum(spread(mine, FAR, 4), axis=0)
        mine, momentum_cols = lax.optimization_barrier((mine, momentum_cols))
        sketch = spread(mine, NEAR, 16).reshape(128, rank)[:cols] / GROUPS
    with jax.named_scope("decode"):
        decoded = lax.dot_general(
            sketch, gauss, (((1,), (1,)), ((), ())), precision=HIGHEST, preferred_element_type=jnp.float32
        )
        stepped = 0.9 * momentum_cols + decoded
        updated = (base_cols - 0.7 * (decoded + 0.9 * stepped)).astype(jnp.bfloat16)
    with jax.named_scope("weights_y"):
        plane_rows = lax.dynamic_slice_in_dim(decoded, lax.axis_index("zhi") * (held // 2), held // 2, 1)
        high, low = halves(plane_rows.reshape(cols, 4, 2, rows).transpose(1, 2, 0, 3))
        pieces = jnp.concatenate([high, low], axis=3)
        copies = jnp.broadcast_to(updated[None], (4, cols, held))
        sent = jnp.concatenate([copies, wide(pieces[:, 0], 128), wide(pieces[:, 1], 128)], axis=2)
        over_y = lax.all_to_all(sent, "y", 0, 0, tiled=True)
    with jax.named_scope("weights_core"):
        first = lax.axis_index("core") == 0
        kept, given = over_y[:, :, held : held + 128], over_y[:, :, held + 128 :]
        kept, given = jnp.where(first, kept, given), jnp.where(first, given, kept)
        own = jnp.concatenate([over_y[:, :, :held], kept], axis=2)
        other = swap(jnp.concatenate([over_y[:, :, :held], given], axis=2), "core")
        both = in_order(own, other, "core", 1)
        new_weights = both[..., :held].reshape(width, held).T
    with jax.named_scope("new_momentum"):
        back = joined(both[..., held : held + rows], both[..., held + rows : held + 2 * rows])
        new_momentum = 0.9 * momentum + back.reshape(width, rows).T
    return new_weights, new_momentum


def solution(mesh):
    fine = Mesh(mesh.devices.reshape(SIZES), ALL)
    placed = (P(FSDP, None), P(REP, FSDP, None), P(FSDP + REP, None), P(FSDP + REP, None))
    return jax.shard_map(
        shards,
        mesh=fine,
        in_specs=placed,
        out_specs=(P(FSDP, None), P(FSDP + REP, None)),
        check_vma=False,
    )
```

```python
import jax
import jax.numpy as jnp
import numpy as np
from jax import lax
from jax.sharding import Mesh, PartitionSpec as P

REP = ("zhi", "y", "core")
FSDP = ("zm", "zn", "x")
PLANE = ("y", "core")
NEAR = ("zn", "x")
FAR = ("zhi", "zm")
CUT = ("core", "y")
ALL = REP + FSDP
SIZES = (2, 4, 2, 2, 4, 4)
GROUPS = 16
CUTS = 8
CONTRACT = (((1,), (1,)), ((), ()))
HIGHEST = lax.Precision.HIGHEST


def swapped(axis):
    index = np.arange(int(np.prod(SIZES))).reshape(SIZES)
    other = np.flip(index, axis=ALL.index(axis))
    return [(int(a), int(b)) for a, b in zip(index.ravel(), other.ravel())]


def swap(value, axis):
    return lax.ppermute(value, ALL, swapped(axis))


def around_y(value):
    index = np.arange(int(np.prod(SIZES))).reshape(SIZES)
    got = [value]
    for step in (1, 2, 3):
        moved = np.roll(index, -step, axis=ALL.index("y"))
        got.append(lax.ppermute(value, ALL, [(int(a), int(b)) for a, b in zip(index.ravel(), moved.ravel())]))
    return jnp.roll(jnp.stack(got[::-1]), lax.axis_index("y") + 1, axis=0)


def in_order(own, other, axis, at):
    first = lax.axis_index(axis) == 0
    return jnp.stack([jnp.where(first, own, other), jnp.where(first, other, own)], axis=at)


def spread(value, axes, parts):
    return lax.all_to_all(jnp.broadcast_to(value[None], (parts,) + value.shape), axes, 0, 0, tiled=True)


def halves(value):
    high = lax.reduce_precision(value, 8, 7)
    return high.astype(jnp.bfloat16), (value - high).astype(jnp.bfloat16)


def joined(high, low):
    return high.astype(jnp.float32) + low.astype(jnp.float32)


def wide(value, lanes):
    return jnp.pad(value, [(0, 0)] * (value.ndim - 1) + [(0, lanes - value.shape[-1])])


def shards(base_weights, local_weights, momentum, sketch_matrix):
    rows, width = momentum.shape
    rank = sketch_matrix.shape[1]
    cols = width // CUTS
    held = base_weights.shape[0]
    cut = lax.axis_index(CUT)

    with jax.named_scope("sketch_rows_zhi"):
        sketch_pair = in_order(sketch_matrix, swap(sketch_matrix, "zhi"), "zhi", 0)
    with jax.named_scope("local_columns"):
        got = lax.all_to_all(local_weights[0].T.reshape(CUTS, cols, held), CUT, 0, 0, tiled=True)
    with jax.named_scope("sketch_rows_plane"):
        gathered = lax.all_gather(sketch_pair.reshape(2 * rows, rank), PLANE, axis=0, tiled=False)
        gauss = gathered.reshape(CUTS, 2, rows, rank).transpose(1, 0, 2, 3).reshape(held, rank)
    with jax.named_scope("drift"):
        base_cols = lax.dynamic_slice_in_dim(base_weights.T, cut * cols, cols, 0).astype(jnp.float32)
        drift = jnp.sum(base_cols[None] - got.astype(jnp.float32), axis=0)
    with jax.named_scope("partial_sketch"):
        partial = jnp.dot(drift, gauss.astype(jnp.float32), precision=HIGHEST, preferred_element_type=jnp.float32)
    with jax.named_scope("sketch_sum"):
        padded = jnp.pad(partial, ((0, 128 - cols), (0, 0)))
        mine = jnp.sum(lax.all_to_all(padded.reshape(16, 8, rank), NEAR, 0, 0, tiled=True), axis=0)
        mine, late = lax.optimization_barrier((mine, momentum))
        small = (late * 8192.0).astype(jnp.float16)
        momentum_pair = in_order(small, swap(small, "zhi"), "zhi", 0)
        momentum_y = around_y(momentum_pair.reshape(2 * rows, width))
        mine = jnp.sum(spread(mine, FAR, 4), axis=0)
        sketch = spread(mine, NEAR, 16).reshape(128, rank)[:cols] / GROUPS
    sketch, momentum_y = lax.optimization_barrier((sketch, momentum_y))
    with jax.named_scope("momentum_core"):
        momentum_all = in_order(momentum_y, swap(momentum_y, "core"), "core", 1)
    with jax.named_scope("prior"):
        known = momentum_all.reshape(CUTS, 2, rows, width).transpose(1, 0, 2, 3).reshape(held, width)
        prior = base_weights.T.astype(jnp.float32) - (0.567 / 8192.0) * known.T.astype(jnp.float32)
    with jax.named_scope("sketch_y"):
        half = spread(sketch, "y", 4)
        half, prior = lax.optimization_barrier((half, prior))
        half = jnp.concatenate(halves(half.reshape(width // 2, rank)), axis=1)
    with jax.named_scope("sketch_core"):
        half_other = swap(half, "core")
    with jax.named_scope("decode"):
        here = lax.axis_index("core") * (width // 2)
        there = width // 2 - here
        twice = jnp.concatenate([gauss, gauss], axis=1)
        own_twice = jnp.concatenate([sketch_matrix, sketch_matrix], axis=1)
        turned = jnp.zeros((width, held), jnp.bfloat16)
        rows_own = []
        for part, start in ((half, here), (half_other, there)):
            decoded = lax.dot_general(part, twice, CONTRACT, preferred_element_type=jnp.float32)
            piece = lax.dynamic_slice_in_dim(prior, start, width // 2, 0) - 1.33 * decoded
            turned = lax.dynamic_update_slice_in_dim(turned, piece.astype(jnp.bfloat16), start, 0)
            rows_own.append(lax.dot_general(own_twice, part, CONTRACT, preferred_element_type=jnp.float32))
        new_weights = turned.T
    with jax.named_scope("new_momentum"):
        first = lax.axis_index("core") == 0
        left, right = jnp.where(first, rows_own[0], rows_own[1]), jnp.where(first, rows_own[1], rows_own[0])
        new_momentum = 0.9 * momentum + jnp.concatenate([left, right], axis=1)
    return new_weights, new_momentum


def solution(mesh):
    fine = Mesh(mesh.devices.reshape(SIZES), ALL)
    placed = (P(FSDP, None), P(REP, FSDP, None), P(FSDP + REP, None), P(FSDP + REP, None))
    return jax.shard_map(
        shards,
        mesh=fine,
        in_specs=placed,
        out_specs=(P(FSDP, None), P(FSDP + REP, None)),
        check_vma=False,
    )
```

```python
import jax
import jax.numpy as jnp
import numpy as np
from jax import lax
from jax.sharding import Mesh, PartitionSpec as P

REP = ("zhi", "y", "core")
FSDP = ("zm", "zn", "x")
PLANE = ("y", "core")
NEAR = ("zn", "x")
FAR = ("zhi", "zm")
CUT = ("core", "y")
ALL = REP + FSDP
SIZES = (2, 4, 2, 2, 4, 4)
GROUPS = 16
CUTS = 8
CONTRACT = (((1,), (1,)), ((), ()))
HIGHEST = lax.Precision.HIGHEST


def swapped(axis):
    index = np.arange(int(np.prod(SIZES))).reshape(SIZES)
    other = np.flip(index, axis=ALL.index(axis))
    return [(int(a), int(b)) for a, b in zip(index.ravel(), other.ravel())]


def swap(value, axis):
    return lax.ppermute(value, ALL, swapped(axis))


def around_y(value):
    index = np.arange(int(np.prod(SIZES))).reshape(SIZES)
    got = [value]
    for step in (1, 2, 3):
        moved = np.roll(index, -step, axis=ALL.index("y"))
        got.append(lax.ppermute(value, ALL, [(int(a), int(b)) for a, b in zip(index.ravel(), moved.ravel())]))
    return jnp.roll(jnp.stack(got[::-1]), lax.axis_index("y") + 1, axis=0)


def in_order(own, other, axis, at):
    first = lax.axis_index(axis) == 0
    return jnp.stack([jnp.where(first, own, other), jnp.where(first, other, own)], axis=at)


def spread(value, axes, parts):
    return lax.all_to_all(jnp.broadcast_to(value[None], (parts,) + value.shape), axes, 0, 0, tiled=True)


def halves(value):
    high = lax.reduce_precision(value, 8, 7)
    return high.astype(jnp.bfloat16), (value - high).astype(jnp.bfloat16)


def joined(high, low):
    return high.astype(jnp.float32) + low.astype(jnp.float32)


def wide(value, lanes):
    return jnp.pad(value, [(0, 0)] * (value.ndim - 1) + [(0, lanes - value.shape[-1])])


def shards(base_weights, local_weights, momentum, sketch_matrix):
    rows, width = momentum.shape
    rank = sketch_matrix.shape[1]
    cols = width // CUTS
    held = base_weights.shape[0]
    cut = lax.axis_index(CUT)

    with jax.named_scope("sketch_rows_zhi"):
        sketch_pair = in_order(sketch_matrix, swap(sketch_matrix, "zhi"), "zhi", 0)
    with jax.named_scope("local_columns"):
        got = lax.all_to_all(local_weights[0].T.reshape(CUTS, cols, held), CUT, 0, 0, tiled=True)
    with jax.named_scope("sketch_rows_plane"):
        gathered = lax.all_gather(sketch_pair.reshape(2 * rows, rank), PLANE, axis=0, tiled=False)
        gauss = gathered.reshape(CUTS, 2, rows, rank).transpose(1, 0, 2, 3).reshape(held, rank)
    with jax.named_scope("drift"):
        base_cols = lax.dynamic_slice_in_dim(base_weights.T, cut * cols, cols, 0).astype(jnp.float32)
        drift = jnp.sum(base_cols[None] - got.astype(jnp.float32), axis=0)
    with jax.named_scope("partial_sketch"):
        partial = jnp.dot(drift, gauss.astype(jnp.float32), precision=HIGHEST, preferred_element_type=jnp.float32)
    with jax.named_scope("sketch_sum"):
        padded = jnp.pad(partial, ((0, 128 - cols), (0, 0)))
        mine = jnp.sum(lax.all_to_all(padded.reshape(16, 8, rank), NEAR, 0, 0, tiled=True), axis=0)
        mine, late = lax.optimization_barrier((mine, momentum))
        small = (late * 8192.0).astype(jnp.float16)
        momentum_pair = in_order(small, swap(small, "zhi"), "zhi", 0)
        momentum_y = around_y(momentum_pair.reshape(2 * rows, width))
        mine = jnp.sum(spread(mine, FAR, 4), axis=0)
        sketch = spread(mine, NEAR, 16).reshape(128, rank)[:cols] / GROUPS
    with jax.named_scope("sketch_y"):
        copies = jnp.concatenate(halves(sketch), axis=1)
        copies = jnp.broadcast_to(copies[None], (4,) + copies.shape)
        copies, momentum_y = lax.optimization_barrier((copies, momentum_y))
    with jax.named_scope("momentum_core"):
        momentum_all = in_order(momentum_y, swap(momentum_y, "core"), "core", 1)
    with jax.named_scope("prior"):
        known = momentum_all.reshape(CUTS, 2, rows, width).transpose(1, 0, 2, 3).reshape(held, width)
        prior = base_weights.T.astype(jnp.float32) - (0.567 / 8192.0) * known.T.astype(jnp.float32)
    with jax.named_scope("sketch_y"):
        half = lax.all_to_all(copies, "y", 0, 0, tiled=True)
        half, prior = lax.optimization_barrier((half, prior))
        half = half.reshape(width // 2, 2 * rank)
    with jax.named_scope("sketch_core"):
        half_other = swap(half, "core")
    with jax.named_scope("decode"):
        here = lax.axis_index("core") * (width // 2)
        there = width // 2 - here
        twice = jnp.concatenate([gauss, gauss], axis=1)
        own_twice = jnp.concatenate([sketch_matrix, sketch_matrix], axis=1)
        turned = jnp.zeros((width, held), jnp.bfloat16)
        rows_own = []
        for part, start in ((half, here), (half_other, there)):
            decoded = lax.dot_general(part, twice, CONTRACT, preferred_element_type=jnp.float32)
            piece = lax.dynamic_slice_in_dim(prior, start, width // 2, 0) - 1.33 * decoded
            turned = lax.dynamic_update_slice_in_dim(turned, piece.astype(jnp.bfloat16), start, 0)
            rows_own.append(lax.dot_general(own_twice, part, CONTRACT, preferred_element_type=jnp.float32))
        new_weights = turned.T
    with jax.named_scope("new_momentum"):
        rows_own = lax.optimization_barrier(rows_own)
        first = lax.axis_index("core") == 0
        left, right = jnp.where(first, rows_own[0], rows_own[1]), jnp.where(first, rows_own[1], rows_own[0])
        new_momentum = 0.9 * momentum + jnp.concatenate([left, right], axis=1)
    return new_weights, new_momentum


def solution(mesh):
    fine = Mesh(mesh.devices.reshape(SIZES), ALL)
    placed = (P(FSDP, None), P(REP, FSDP, None), P(FSDP + REP, None), P(FSDP + REP, None))
    return jax.shard_map(
        shards,
        mesh=fine,
        in_specs=placed,
        out_specs=(P(FSDP, None), P(FSDP + REP, None)),
        check_vma=False,
    )
```
